128 devices in a mesh: row: 8 (over y, z_hi), col: 16 (over z_lo, x, core).
Axes of the slice: x: 4, y: 4, z: 4 (z_hi: 2, z_lo: 2; z = z_hi * 2 + z_lo), core: 2. Of those that a mesh axis runs over, the one named last changes fastest.
Arguments:
- features: bfloat16 [65536, 128], P(('row', 'col')), may hold values from -6 to 6
- cotangent: bfloat16 [65536, 256], P(('row', 'col')), may hold values from -6 to 6
- w_self1: bfloat16 [128, 256], replicated, may hold values from -0.5 to 0.5
- w_neigh1: bfloat16 [128, 256], replicated, may hold values from -0.5 to 0.5
- w_self2: bfloat16 [256, 256], replicated, may hold values from -0.375 to 0.375
- w_neigh2: bfloat16 [256, 256], replicated, may hold values from -0.375 to 0.375
- tile_rows: int32 [8, 16, 448], P('row', 'col'), may hold values from 0 to 63, as said below
- tile_cols: int32 [8, 16, 448], P('row', 'col'), may hold values from 0 to 31, as said below
- tile_values: bfloat16 [8, 16, 448, 128, 128], P('row', 'col'), may hold values from -0.046875 to 0.046875
- tile_live: int32 [8, 16], P('row', 'col'), may hold values from 112 to 448, as said below
Outputs:
- output: bfloat16 [65536, 256], P(('row', 'col'))
- grad_self1: float32 [128, 256], replicated
- grad_neigh1: float32 [128, 256], replicated
- grad_self2: float32 [256, 256], replicated
- grad_neigh2: float32 [256, 256], replicated
The draws below stay inside these ranges and needn't reach their ends.
Inputs may be any that keep to these rules, and one draw needn't show every extreme that they name: `tile_rows`: on each device the 448 slots name distinct tiles; block rows lie in the device's row group of 16 * 4 blocks. `tile_cols`: block columns lie in the device's column group of 8 * 4 blocks. Slots from tile_live on are not part of the adjacency; some device has all 448 slots live.
All inputs are finite; a program needn't handle non-finite values.
Results may differ from the reference program's by a relative error of at most 0.0049.
Values may be sent and summed in bfloat16 or wider, within the bound.
No kernel may reach another device: no remote copies, remote signals or barrier semaphores. Data moves between devices by JAX's collectives and lax.ppermute only.
A program may use at most 128 MiB of HBM per device.

```python
import jax
import jax.numpy as jnp
from jax import lax

F = 128
H = 256
BLOCK = 128
SEG = 4
TILES_DEV = 448
NODES = 65536
N_ROW = 8
N_COL = 16


def tile_places(key):
    device_keys = jax.random.split(key, N_ROW * N_COL)
    positions = N_COL * SEG * N_ROW * SEG
    chosen = jax.vmap(lambda one_key: jax.random.permutation(one_key, positions)[:TILES_DEV])(device_keys)
    return chosen.reshape(N_ROW, N_COL, TILES_DEV).astype(jnp.int32)


def draw_tile_rows(key, part):
    places = tile_places(key)
    return (places // (N_ROW * SEG)).astype(jnp.int32)


def draw_tile_cols(key, part):
    places = tile_places(key)
    return (places % (N_ROW * SEG)).astype(jnp.int32)


def draw_tile_live(key, part):
    key = jax.random.fold_in(key, 3)
    first_key, second_key = jax.random.split(key)
    counts = jax.random.randint(first_key, (N_ROW * N_COL,), TILES_DEV // 4, TILES_DEV + 1)
    full_device = jax.random.randint(second_key, (), 0, N_ROW * N_COL)
    flattened = jnp.where(jnp.arange(N_ROW * N_COL) == full_device, TILES_DEV, counts)
    return flattened.reshape(N_ROW, N_COL).astype(jnp.int32)


def level_of(own_key, extent, pieces, low, top_value):
    gain = 1.0
    for dim, blocks in pieces:
        heights = jax.random.uniform(jax.random.fold_in(jax.random.fold_in(own_key, 6), dim), (blocks,), jnp.float32, low / len(pieces), top_value / len(pieces))
        gain = gain * jnp.repeat(jnp.exp(heights), extent[dim] // blocks).reshape((-1,) + (1,) * (len(extent) - 1 - dim))
    return gain


def noise(key, extent, spread, limit, cuts=(), kind=jnp.bfloat16):
    values = jax.random.normal(key, extent, jnp.float32) * spread
    if len(cuts) > 0:
        values = level_of(key, extent, cuts, -0.22, 0.18) * values
    return jnp.clip(values, min=-limit, max=limit).astype(kind)


def setup_inputs(seed: int = 0) -> dict:
    splits = jax.random.split(jax.random.key(seed), 11)
    features = noise(splits[0], (NODES, F), 1.0, 6.0, ((0, 128),))
    cotangent = noise(splits[1], (NODES, H), 1.0, 6.0, ((0, 128),))
    w_self1 = noise(splits[2], (F, H), F ** -0.5, 0.5)
    w_neigh1 = noise(splits[3], (F, H), F ** -0.5, 0.5)
    w_self2 = noise(splits[4], (H, H), H ** -0.5, 0.375)
    w_neigh2 = noise(splits[5], (H, H), H ** -0.5, 0.375)
    tile_rows = draw_tile_rows(jax.random.fold_in(splits[10], 71), 0)
    tile_cols = draw_tile_cols(jax.random.fold_in(splits[10], 71), 0)
    tile_values = noise(splits[8], (N_ROW, N_COL, TILES_DEV, BLOCK, BLOCK), (BLOCK * TILES_DEV // SEG) ** -0.5, 0.046875, ((0, 8), (1, 16)))
    tile_live = draw_tile_live(jax.random.fold_in(splits[10], 71), 0)
    return {"features": features, "cotangent": cotangent, "w_self1": w_self1, "w_neigh1": w_neigh1, "w_self2": w_self2, "w_neigh2": w_neigh2, "tile_rows": tile_rows, "tile_cols": tile_cols, "tile_values": tile_values, "tile_live": tile_live}


def tile_apply(source, tile_rows, tile_cols, tile_values, tile_live, width, transpose):
    blocks = source.reshape(-1, BLOCK, width).astype(jnp.float32)
    slots = jnp.arange(TILES_DEV, dtype=jnp.int32)

    def one_device(carry, device):
        row_index = device // N_COL
        col_index = device % N_COL
        rows_here = tile_rows[row_index, col_index]
        cols_here = tile_cols[row_index, col_index]
        values = tile_values[row_index, col_index].astype(jnp.float32)
        global_row = (row_index * N_COL * SEG + rows_here).astype(jnp.int32)
        global_col = (((cols_here // SEG) * N_COL + col_index) * SEG + cols_here % SEG).astype(jnp.int32)
        valid = (slots < tile_live[row_index, col_index]).astype(jnp.float32)
        if transpose:
            product = jnp.einsum("tji,tjw->tiw", values, blocks[global_row])
            target = global_col
        else:
            product = jnp.einsum("tij,tjw->tiw", values, blocks[global_col])
            target = global_row
        product = product * valid[:, None, None]
        return carry.at[target].add(product), None

    start = jnp.zeros((NODES // BLOCK, BLOCK, width), jnp.float32)
    total, unused = lax.scan(one_device, start, jnp.arange(N_ROW * N_COL, dtype=jnp.int32))
    return total.reshape(NODES, width)


def fdot(left, right):
    return jnp.dot(left.astype(jnp.float32), right.astype(jnp.float32), precision=lax.Precision.HIGHEST, preferred_element_type=jnp.float32)


def reference(features, cotangent, w_self1, w_neigh1, w_self2, w_neigh2, tile_rows, tile_cols, tile_values, tile_live):
    agg1 = tile_apply(features, tile_rows, tile_cols, tile_values, tile_live, F, False)
    z1 = jnp.dot(features, w_self1, preferred_element_type=jnp.float32) + fdot(agg1, w_neigh1)
    h1 = jax.nn.silu(z1).astype(jnp.bfloat16)
    agg2 = tile_apply(h1, tile_rows, tile_cols, tile_values, tile_live, H, False)
    output = (jnp.dot(h1, w_self2, preferred_element_type=jnp.float32) + fdot(agg2, w_neigh2)).astype(jnp.bfloat16)
    back = tile_apply(cotangent, tile_rows, tile_cols, tile_values, tile_live, H, True)
    dh1 = jnp.dot(cotangent, w_self2.T, preferred_element_type=jnp.float32) + fdot(back, w_neigh2.T)
    sigma = jax.nn.sigmoid(z1)
    dz1 = (dh1 * (sigma + z1 * sigma * (1.0 - sigma))).astype(jnp.bfloat16)
    grad_self2 = jnp.dot(h1.T, cotangent, preferred_element_type=jnp.float32)
    grad_neigh2 = fdot(agg2.T, cotangent)
    grad_self1 = jnp.dot(features.T, dz1, preferred_element_type=jnp.float32)
    grad_neigh1 = fdot(agg1.T, dz1)
    return (output, grad_self1, grad_neigh1, grad_self2, grad_neigh2)
```

```python
import functools

import jax
import jax.numpy as jnp
from jax import lax
from jax.experimental import pallas as pl
from jax.experimental.pallas import tpu as pltpu
from jax.sharding import PartitionSpec as P

BF = jnp.bfloat16
F32 = jnp.float32
UNROLL = 16
GROUP = 64
ROW_ORDER = ((0, 0), (0, 1), (3, 0), (1, 0), (3, 1), (1, 1), (2, 0), (2, 1))
COL_ORDER = tuple((dx, dz) for dx in range(4) for dz in range(2))


def row_perm(dy, dz):
    return [(y * 2 + h, ((y + dy) % 4) * 2 + (h ^ dz)) for y in range(4) for h in range(2)]


def col_perm(dx, dz, dc):
    return [
        ((z * 4 + x) * 2 + c, ((z ^ dz) * 4 + (x + dx) % 4) * 2 + (c ^ dc))
        for z in range(2)
        for x in range(4)
        for c in range(2)
    ]


def send_row(value, dy, dz):
    return lax.ppermute(value, "row", row_perm(dy, dz))


def send_col(value, dx, dz, dc=0):
    return lax.ppermute(value, "col", col_perm(dx, dz, dc))


def gather_row(value):
    half = value.shape[0] // 2
    flip = send_row(value, 0, 1)
    below = send_row(value, 1, 0)
    above = send_row(value, 3, 0)
    flip_below = send_row(flip, 1, 0)
    flip_above = send_row(flip, 3, 0)
    far_a = send_row(below[:half], 1, 0)
    far_b = send_row(above[half:], 3, 0)
    flip_far_a = send_row(flip_below[:half], 1, 0)
    flip_far_b = send_row(flip_above[half:], 3, 0)
    return [value, flip, below, above, flip_below, flip_above, far_a, far_b, flip_far_a, flip_far_b]


def tile_kernel(groups, transpose, n_pieces, splits, *refs):
    src, dst, turns = refs[:3]
    pieces = refs[3 : 3 + n_pieces]
    values = refs[3 + n_pieces]
    outs = refs[4 + n_pieces : 4 + n_pieces + len(splits)]
    held, total, sems = refs[4 + n_pieces + len(splits) :]
    g = pl.program_id(0)

    @pl.when(g == 0)
    def _():
        copies = []
        at = 0
        for k, piece in enumerate(pieces):
            rows = piece.shape[0]
            copy = pltpu.make_async_copy(piece, held.at[pl.ds(at, rows)], sems.at[k])
            copy.start()
            copies.append(copy)
            at += rows
        total[...] = jnp.zeros_like(total)
        for copy in copies:
            copy.wait()

    per_group = GROUP // UNROLL
    steps = jnp.clip(turns[0] - g * per_group, 0, per_group)

    def body(i, carry):
        for u in range(UNROLL):
            t = i * UNROLL + u
            s = src[g * GROUP + t]
            d = dst[g * GROUP + t]
            dims = (((0,), (0,)), ((), ())) if transpose else (((1,), (0,)), ((), ()))
            total[d] += lax.dot_general(values[t], held[s], dims, preferred_element_type=F32)
        return carry

    lax.fori_loop(0, steps, body, 0)

    @pl.when(g == groups - 1)
    def _():
        at = 0
        for out, (count, _) in zip(outs, splits):
            out[...] = total[at : at + count].astype(out.dtype)
            at += count


def tile_product(src, dst, turns, pieces, values, splits, transpose, name):
    slots, block, _ = values.shape
    width = pieces[0].shape[-1]
    pieces = [piece.reshape(-1, block, width) for piece in pieces]
    n_src = sum(piece.shape[0] for piece in pieces)
    n_dst = sum(count for count, _ in splits)
    groups = slots // GROUP
    per_group = GROUP // UNROLL

    def value_map(g, src, dst, turns):
        last = jnp.maximum((turns[0] + per_group - 1) // per_group - 1, 0)
        return (jnp.minimum(g, last), 0, 0)

    whole = lambda g, src, dst, turns: (0, 0, 0)
    return pl.pallas_call(
        functools.partial(tile_kernel, groups, transpose, len(pieces), splits),
        grid_spec=pltpu.PrefetchScalarGridSpec(
            num_scalar_prefetch=3,
            grid=(groups,),
            in_specs=[pl.BlockSpec(memory_space=pl.ANY)] * len(pieces)
            + [pl.BlockSpec((GROUP, block, block), value_map)],
            out_specs=[pl.BlockSpec((count, block, width), whole) for count, _ in splits],
            scratch_shapes=[
                pltpu.VMEM((n_src, block, width), BF),
                pltpu.VMEM((n_dst + 1, block, width), F32),
                pltpu.SemaphoreType.DMA((len(pieces),)),
            ],
        ),
        out_shape=[jax.ShapeDtypeStruct((count, block, width), kind) for count, kind in splits],
        compiler_params=pltpu.CompilerParams(vmem_limit_bytes=56 << 20),
        cost_estimate=pl.CostEstimate(flops=18_000_000_000, bytes_accessed=20 << 20, transcendentals=0),
        name=name,
    )(src, dst, turns, *pieces, values)


def scatter_col(own, other):
    width = own.shape[-1]
    got = send_col(other, 0, 0, 1)
    sums = {}
    for k in (4, 5, 2, 3, 6, 7, 1, 0):
        part = own[4 * k : 4 * k + 4] + got[4 * k : 4 * k + 4].astype(F32)
        sums[k] = part if k == 0 else send_col(part.astype(BF), *COL_ORDER[k])
    total = sums[0]
    for k in range(1, 8):
        total = total + sums[k].astype(F32)
    return total.reshape(-1, width)


def scatter_row(parts):
    width = parts[0].shape[-1]
    total = parts[0]
    got = {k: send_row(parts[k], *ROW_ORDER[k]) for k in (6, 7, 4, 5, 2, 3, 1)}
    for k in range(1, 8):
        total = total + got[k].astype(F32)
    return total.reshape(-1, width)


def sum_all(value, y, x, core):
    rows, width = value.shape

    def pick(parts, i):
        return lax.dynamic_index_in_dim(parts, i, 0, False)

    def scatter(part, send, i):
        parts = part.reshape(4, -1, width)
        total = pick(parts, i)
        for d in (1, 2, 3):
            total = total + send(pick(parts, (i + d) % 4), d, 0)
        return total

    def gather(part, send, i):
        parts = jnp.stack([part] + [send(part, d, 0) for d in (1, 2, 3)])
        out = jnp.concatenate([pick(parts, (i - j) % 4) for j in range(4)])
        return out

    halves = value.reshape(2, rows // 2, width)
    part = pick(halves, core) + send_col(pick(halves, 1 - core), 0, 0, 1)
    part = scatter(part, send_col, x)
    part = scatter(part, send_row, y)
    part = part + send_row(part, 0, 1)
    part = part + send_col(part, 0, 1)
    part = gather(part, send_row, y)
    part = gather(part, send_col, x)
    other = send_col(part, 0, 0, 1)
    first = jnp.where(core == 0, part, other)
    second = jnp.where(core == 0, other, part)
    return jnp.concatenate([first, second])


def fdot(left, right):
    return jnp.dot(left, right.astype(F32), precision=lax.Precision.HIGHEST, preferred_element_type=F32)


def local(
    features,
    cotangent,
    w_self1,
    w_neigh1,
    w_self2,
    w_neigh2,
    tile_rows,
    tile_cols,
    tile_values,
    tile_live,
):
    values = tile_values[0, 0]
    slots = values.shape[0]
    live = tile_live[0, 0]
    rows_here = tile_rows[0, 0]
    cols_here = tile_cols[0, 0]
    row_at = lax.axis_index("row")
    col_at = lax.axis_index("col")
    y, z_hi = row_at // 2, row_at % 2
    z_lo, x, core = col_at // 8, (col_at // 2) % 4, col_at % 2

    owner = cols_here // 4
    dy = (owner // 2 - y) % 4
    dz = (owner % 2) ^ z_hi
    place = jnp.where(dy == 0, dz, jnp.where(dy == 3, 2 + 2 * dz, jnp.where(dy == 1, 3 + 2 * dz, 6 + dz)))
    col_place = place * 4 + cols_here % 4
    owner = rows_here // 4
    dx = ((owner // 2) % 4 - x) % 4
    dz = (owner // 8) ^ z_lo
    row_place = ((owner % 2) ^ core) * 32 + (dx * 2 + dz) * 4 + rows_here % 4
    alive = jnp.arange(slots, dtype=jnp.int32) < live
    row_target = jnp.where(alive, row_place, 64)
    col_target = jnp.where(alive, col_place, 32)
    turns = ((live + UNROLL - 1) // UNROLL).reshape(1)

    forward_splits = ((32, F32), (32, BF))
    back_splits = ((4, F32),) + ((4, BF),) * 7

    gathered_c = lax.all_gather(cotangent, "col", axis=0, tiled=True)
    gathered_x = gather_row(features)
    own, other = tile_product(
        col_place, row_target, turns, gathered_x, values, forward_splits, False, "neighbour_sum_one"
    )
    back_parts = tile_product(
        rows_here, col_target, turns, [gathered_c], values, back_splits, True, "neighbour_sum_back"
    )
    agg1 = scatter_col(own, other)
    z1 = jnp.dot(features, w_self1, preferred_element_type=F32) + fdot(agg1, w_neigh1)
    h1 = jax.nn.silu(z1).astype(BF)
    gathered_h = gather_row(h1)
    own, other = tile_product(
        col_place, row_target, turns, gathered_h, values, forward_splits, False, "neighbour_sum_two"
    )
    back = scatter_row(back_parts)
    dh1 = jnp.dot(cotangent, w_self2.T, preferred_element_type=F32) + fdot(back, w_neigh2.T)
    sigma = jax.nn.sigmoid(z1)
    dz1 = (dh1 * (sigma + z1 * sigma * (1.0 - sigma))).astype(BF)
    local_self2 = jnp.dot(h1.T, cotangent, preferred_element_type=F32)
    local_neigh2 = jnp.dot(
        h1.T.astype(F32), back, precision=lax.Precision.HIGHEST, preferred_element_type=F32
    )
    local_self1 = jnp.dot(features.T, dz1, preferred_element_type=F32)
    local_neigh1 = fdot(agg1.T, dz1)
    grads = sum_all(jnp.concatenate([local_self1, local_neigh1, local_self2, local_neigh2]), y, x, core)
    agg2 = scatter_col(own, other)
    output = (jnp.dot(h1, w_self2, preferred_element_type=F32) + fdot(agg2, w_neigh2)).astype(BF)
    return (output, grads[:128], grads[128:256], grads[256:512], grads[512:])


def solution(mesh):
    return jax.shard_map(
        local,
        mesh=mesh,
        in_specs=(
            P(("row", "col"), None),
            P(("row", "col"), None),
            P(),
            P(),
            P(),
            P(),
            P("row", "col", None),
            P("row", "col", None),
            P("row", "col", None, None, None),
            P("row", "col"),
        ),
        out_specs=(P(("row", "col"), None), P(), P(), P(), P()),
        check_vma=False,
    )
```

```python
import functools

import jax
import jax.numpy as jnp
from jax import lax
from jax.experimental import pallas as pl
from jax.experimental.pallas import tpu as pltpu
from jax.sharding import PartitionSpec as P

BF = jnp.bfloat16
F32 = jnp.float32
UNROLL = 56
DEPTH = 3


def row_perm(dy, dz):
    return [(y * 2 + h, ((y + dy) % 4) * 2 + (h ^ dz)) for y in range(4) for h in range(2)]


def col_perm(dx, dz, dc):
    return [
        ((z * 4 + x) * 2 + c, ((z ^ dz) * 4 + (x + dx) % 4) * 2 + (c ^ dc))
        for z in range(2)
        for x in range(4)
        for c in range(2)
    ]


def send_both_z(value):
    pairs = [(r * 16 + c, (r ^ 1) * 16 + (c ^ 8)) for r in range(8) for c in range(16)]
    return lax.ppermute(value, ("row", "col"), pairs)


def send_row(value, dy, dz):
    return lax.ppermute(value, "row", row_perm(dy, dz))


def send_col(value, dx, dz, dc=0):
    return lax.ppermute(value, "col", col_perm(dx, dz, dc))


def gather_row(value):
    pair = jnp.concatenate([value, send_row(value, 0, 1)])
    far, below, above = [send_row(pair, dy, 0) for dy in (2, 1, 3)]
    return [pair, below, above, far]


def tile_kernel(transpose, n_pieces, splits, *refs):
    src, dst, turns = refs[:3]
    pieces = refs[3 : 3 + n_pieces]
    values = refs[3 + n_pieces]
    outs = refs[4 + n_pieces : 4 + n_pieces + len(splits)]
    held, ring, total, rounded, piece_sems, ring_sems, out_sems = refs[4 + n_pieces + len(splits) :]
    count = turns[0]

    def fetch(turn, slot):
        return pltpu.make_async_copy(
            values.at[pl.ds(turn * UNROLL, UNROLL)], ring.at[pl.ds(slot * UNROLL, UNROLL)], ring_sems.at[slot]
        )

    copies = []
    at = 0
    for k, piece in enumerate(pieces):
        copy = pltpu.make_async_copy(piece, held.at[pl.ds(at, piece.shape[0])], piece_sems.at[k])
        copy.start()
        copies.append(copy)
        at += piece.shape[0]
    for slot in range(DEPTH):

        @pl.when(slot < count)
        def _():
            fetch(slot, slot).start()

    def clear(i, carry):
        total[i] = jnp.zeros(total.shape[1:], F32)
        return carry

    lax.fori_loop(0, total.shape[0], clear, 0)
    for copy in copies:
        copy.wait()

    def body(turn, carry):
        slot = lax.rem(turn, DEPTH)
        fetch(turn, slot).wait()
        for u in range(UNROLL):
            s = src[turn * UNROLL + u]
            d = dst[turn * UNROLL + u]
            dims = (((0,), (0,)), ((), ())) if transpose else (((1,), (0,)), ((), ()))
            total[d] += lax.dot_general(ring[slot * UNROLL + u], held[s], dims, preferred_element_type=F32)

        @pl.when(turn + DEPTH < count)
        def _():
            fetch(turn + DEPTH, slot).start()

        return carry

    lax.fori_loop(0, count, body, 0)

    copies = []
    at = 0
    for k, (out, (blocks, kind)) in enumerate(zip(outs, splits)):
        if kind == F32:
            copies.append(pltpu.make_async_copy(total.at[pl.ds(at, blocks)], out, out_sems.at[k]))
            copies[-1].start()
        at += blocks
    at = 0
    to = 0
    for k, (out, (blocks, kind)) in enumerate(zip(outs, splits)):
        if kind != F32:

            def cast(i, carry, at=at, to=to):
                rounded[to + i] = total[at + i].astype(BF)
                return carry

            lax.fori_loop(0, blocks, cast, 0)
            copies.append(pltpu.make_async_copy(rounded.at[pl.ds(to, blocks)], out, out_sems.at[k]))
            copies[-1].start()
            to += blocks
        at += blocks
    for copy in copies:
        copy.wait()


def tile_product(src, dst, turns, pieces, values, splits, transpose, name, vmem=40 << 20):
    _, block, _ = values.shape
    width = pieces[0].shape[-1]
    pieces = [piece.reshape(-1, block, width) for piece in pieces]
    n_src = sum(piece.shape[0] for piece in pieces)
    n_dst = sum(count for count, _ in splits)
    n_rounded = sum(count for count, kind in splits if kind != F32)
    anywhere = pl.BlockSpec(memory_space=pl.ANY)
    return pl.pallas_call(
        functools.partial(tile_kernel, transpose, len(pieces), splits),
        grid_spec=pltpu.PrefetchScalarGridSpec(
            num_scalar_prefetch=3,
            grid=(1,),
            in_specs=[anywhere] * (len(pieces) + 1),
            out_specs=[anywhere] * len(splits),
            scratch_shapes=[
                pltpu.VMEM((n_src, block, width), BF),
                pltpu.VMEM((DEPTH * UNROLL, block, block), BF),
                pltpu.VMEM((n_dst + 1, block, width), F32),
                pltpu.VMEM((n_rounded, block, width), BF),
                pltpu.SemaphoreType.DMA((len(pieces),)),
                pltpu.SemaphoreType.DMA((DEPTH,)),
                pltpu.SemaphoreType.DMA((len(splits),)),
            ],
        ),
        out_shape=[jax.ShapeDtypeStruct((count, block, width), kind) for count, kind in splits],
        compiler_params=pltpu.CompilerParams(vmem_limit_bytes=vmem),
        cost_estimate=pl.CostEstimate(flops=18_000_000_000, bytes_accessed=20 << 20, transcendentals=0),
        name=name,
    )(src, dst, turns, *pieces, values)


def add_cores(own, other):
    width = own.shape[-1]

    def part(d):
        return (own[8 * d : 8 * d + 8] + other[8 * d : 8 * d + 8].astype(F32)).reshape(-1, width)

    return part(0), [part(d).astype(BF) for d in (2, 1, 3)]


def send_x(parts):
    return [send_col(part, d, 0) for part, d in zip(parts, (2, 1, 3))]


def add_x(own, sent):
    total = own + sent[0].astype(F32) + sent[1].astype(F32) + sent[2].astype(F32)
    return total.reshape(2, -1, total.shape[-1])


def add_z(halves):
    return halves[0] + send_col(halves[1].astype(BF), 0, 1).astype(F32)


def add_z_hi(own, sent):
    other = jnp.concatenate(sent).astype(F32)
    return (own + other).reshape(4, -1, own.shape[-1])


def sum_y(parts):
    sent = [send_row(parts[d].astype(BF), d, 0) for d in (2, 1, 3)]
    return parts[0] + sent[0].astype(F32) + sent[1].astype(F32) + sent[2].astype(F32)


def pick(parts, i):
    return lax.dynamic_index_in_dim(parts, i, 0, False)


def sum_cores(value, core):
    halves = value.reshape(2, -1, value.shape[-1])
    return pick(halves, core) + send_col(pick(halves, 1 - core), 0, 0, 1)


def scatter_x(part, x):
    parts = part.reshape(4, -1, part.shape[-1])
    sent = [send_col(pick(parts, (x + d) % 4), d, 0) for d in (2, 1, 3)]
    return pick(parts, x) + sent[0] + sent[1] + sent[2]


def exchange_y(part):
    far, above, below = [send_row(part, d, 0) for d in (2, 1, 3)]
    return (part + far) + (above + below)


def exchange_z(part):
    high, low, both = send_row(part, 0, 1), send_col(part, 0, 1), send_both_z(part)
    return (part + high) + (low + both)


def gather_x(part, x):
    far, above, below = [send_col(part, d, 0) for d in (2, 1, 3)]
    parts = jnp.stack([part, above, far, below])
    return jnp.concatenate([pick(parts, (x - j) % 4) for j in range(4)])


def fdot(left, right):
    return jnp.dot(left, right.astype(F32), precision=lax.Precision.HIGHEST, preferred_element_type=F32)


def local(
    features,
    cotangent,
    w_self1,
    w_neigh1,
    w_self2,
    w_neigh2,
    tile_rows,
    tile_cols,
    tile_values,
    tile_live,
):
    values = tile_values[0, 0]
    slots = values.shape[0]
    live = tile_live[0, 0]
    rows_here = tile_rows[0, 0]
    cols_here = tile_cols[0, 0]
    row_at = lax.axis_index("row")
    col_at = lax.axis_index("col")
    y, z_hi = row_at // 2, row_at % 2
    z_lo, x, core = col_at // 8, (col_at // 2) % 4, col_at % 2

    owner = cols_here // 4
    dy = (owner // 2 - y) % 4
    dz = (owner % 2) ^ z_hi
    place = jnp.where(dy == 0, 0, jnp.where(dy == 3, 2, jnp.where(dy == 1, 4, 6))) + dz
    col_place = place * 4 + cols_here % 4
    col_sum_place = dz * 16 + dy * 4 + cols_here % 4
    owner = rows_here // 4
    dx = ((owner // 2) % 4 - x) % 4
    dz = (owner // 8) ^ z_lo
    row_place = ((owner % 2) ^ core) * 32 + (dx * 2 + dz) * 4 + rows_here % 4
    alive = jnp.arange(slots, dtype=jnp.int32) < live
    row_target = jnp.where(alive, row_place, 64)
    col_target = jnp.where(alive, col_sum_place, 32)
    turns = ((live + UNROLL - 1) // UNROLL).reshape(1)

    forward_splits = ((32, F32), (32, BF))
    back_splits = ((16, F32), (8, BF), (8, BF))

    gathered_c = lax.all_gather(cotangent, "col", axis=0, tiled=True)
    gathered_x = gather_row(features)
    own, other = tile_product(
        col_place, row_target, turns, gathered_x, values, forward_splits, False, "neighbour_sum_one"
    )
    mine, parts = add_cores(own, send_col(other, 0, 0, 1))
    last, gathered_c = lax.optimization_barrier((parts[2], gathered_c))
    sent = send_x([parts[0], parts[1], last])
    back_own, *back_parts = tile_product(
        rows_here, col_target, turns, [gathered_c], values, back_splits, True, "neighbour_sum_back"
    )
    sent, back_parts = lax.optimization_barrier((sent, back_parts))
    back_parts = [send_row(part, 0, 1) for part in back_parts]
    agg1 = add_z(add_x(mine, sent))
    z1 = jnp.dot(features, w_self1, preferred_element_type=F32) + fdot(agg1, w_neigh1)
    h1 = jax.nn.silu(z1).astype(BF)
    gathered_h = gather_row(h1)
    gathered_h, back_parts = lax.optimization_barrier((gathered_h, back_parts))
    back_parts = add_z_hi(back_own, back_parts)
    gathered_h, back_parts = lax.optimization_barrier((gathered_h, back_parts))
    back = sum_y(back_parts)
    own, other = tile_product(
        col_place, row_target, turns, gathered_h, values, forward_splits, False, "neighbour_sum_two"
    )
    own, other, back = lax.optimization_barrier((own, other, back))
    other = send_col(other, 0, 0, 1)
    dh1 = jnp.dot(cotangent, w_self2.T, preferred_element_type=F32) + fdot(back, w_neigh2.T)
    sigma = jax.nn.sigmoid(z1)
    dz1 = (dh1 * (sigma + z1 * sigma * (1.0 - sigma))).astype(BF)
    local_self2 = jnp.dot(h1.T, cotangent, preferred_element_type=F32)
    local_neigh2 = jnp.dot(
        h1.T.astype(F32), back, precision=lax.Precision.HIGHEST, preferred_element_type=F32
    )
    local_self1 = jnp.dot(features.T, dz1, preferred_element_type=F32)
    local_neigh1 = fdot(agg1.T, dz1)
    grads = jnp.concatenate([local_self1, local_neigh1, local_self2, local_neigh2])
    mine, parts = add_cores(own, other)
    sent = send_x(parts)
    grads = exchange_y(scatter_x(sum_cores(grads, core), x))
    sent, grads = lax.optimization_barrier((sent, grads))
    grads = exchange_z(grads)
    agg2 = add_z(add_x(mine, sent))
    output = (jnp.dot(h1, w_self2, preferred_element_type=F32) + fdot(agg2, w_neigh2)).astype(BF)
    grads = gather_x(grads, x)
    other = send_col(grads, 0, 0, 1)
    grads = jnp.where(core == 0, jnp.concatenate([grads, other]), jnp.concatenate([other, grads]))
    return (output, grads[:128], grads[128:256], grads[256:512], grads[512:])


def solution(mesh):
    return jax.shard_map(
        local,
        mesh=mesh,
        in_specs=(
            P(("row", "col"), None),
            P(("row", "col"), None),
            P(),
            P(),
            P(),
            P(),
            P("row", "col", None),
            P("row", "col", None),
            P("row", "col", None, None, None),
            P("row", "col"),
        ),
        out_specs=(P(("row", "col"), None), P(), P(), P(), P()),
        check_vma=False,
    )
```

```python
import functools

import jax
import jax.numpy as jnp
from jax import lax
from jax.experimental import pallas as pl
from jax.experimental.pallas import tpu as pltpu
from jax.sharding import PartitionSpec as P

BF = jnp.bfloat16
F32 = jnp.float32
UNROLL = 56
DEPTH = 3


def row_perm(dy, dz):
    return [(y * 2 + h, ((y + dy) % 4) * 2 + (h ^ dz)) for y in range(4) for h in range(2)]


def col_perm(dx, dz, dc):
    return [
        ((z * 4 + x) * 2 + c, ((z ^ dz) * 4 + (x + dx) % 4) * 2 + (c ^ dc))
        for z in range(2)
        for x in range(4)
        for c in range(2)
    ]


def send_both_z(value):
    pairs = [(r * 16 + c, (r ^ 1) * 16 + (c ^ 8)) for r in range(8) for c in range(16)]
    return lax.ppermute(value, ("row", "col"), pairs)


def send_row(value, dy, dz):
    return lax.ppermute(value, "row", row_perm(dy, dz))


def send_col(value, dx, dz, dc=0):
    return lax.ppermute(value, "col", col_perm(dx, dz, dc))


def gather_row(value):
    pair = jnp.concatenate([value, send_row(value, 0, 1)])
    below, above, far = [send_row(pair, dy, 0) for dy in (1, 3, 2)]
    return [pair, below, above, far]


def tile_kernel(transpose, n_pieces, splits, *refs):
    src, dst, turns = refs[:3]
    pieces = refs[3 : 3 + n_pieces]
    values = refs[3 + n_pieces]
    outs = refs[4 + n_pieces : 4 + n_pieces + len(splits)]
    held, ring, total, rounded, piece_sems, ring_sems, out_sems = refs[4 + n_pieces + len(splits) :]
    count = turns[0]

    def fetch(turn, slot):
        return pltpu.make_async_copy(
            values.at[pl.ds(turn * UNROLL, UNROLL)], ring.at[pl.ds(slot * UNROLL, UNROLL)], ring_sems.at[slot]
        )

    copies = []
    at = 0
    for k, piece in enumerate(pieces):
        copy = pltpu.make_async_copy(piece, held.at[pl.ds(at, piece.shape[0])], piece_sems.at[k])
        copy.start()
        copies.append(copy)
        at += piece.shape[0]
    for slot in range(DEPTH):

        @pl.when(slot < count)
        def _():
            fetch(slot, slot).start()

    def clear(i, carry):
        total[i] = jnp.zeros(total.shape[1:], F32)
        return carry

    lax.fori_loop(0, total.shape[0], clear, 0)
    for copy in copies:
        copy.wait()

    def body(turn, carry):
        slot = lax.rem(turn, DEPTH)
        fetch(turn, slot).wait()
        for u in range(UNROLL):
            s = src[turn * UNROLL + u]
            d = dst[turn * UNROLL + u]
            dims = (((0,), (0,)), ((), ())) if transpose else (((1,), (0,)), ((), ()))
            total[d] += lax.dot_general(ring[slot * UNROLL + u], held[s], dims, preferred_element_type=F32)

        @pl.when(turn + DEPTH < count)
        def _():
            fetch(turn + DEPTH, slot).start()

        return carry

    lax.fori_loop(0, count, body, 0)

    copies = []
    at = 0
    for k, (out, (blocks, kind)) in enumerate(zip(outs, splits)):
        if kind == F32:
            copies.append(pltpu.make_async_copy(total.at[pl.ds(at, blocks)], out, out_sems.at[k]))
            copies[-1].start()
        at += blocks
    at = 0
    to = 0
    for k, (out, (blocks, kind)) in enumerate(zip(outs, splits)):
        if kind != F32:

            def cast(i, carry, at=at, to=to):
                rounded[to + i] = total[at + i].astype(BF)
                return carry

            lax.fori_loop(0, blocks, cast, 0)
            copies.append(pltpu.make_async_copy(rounded.at[pl.ds(to, blocks)], out, out_sems.at[k]))
            copies[-1].start()
            to += blocks
        at += blocks
    for copy in copies:
        copy.wait()


def tile_product(src, dst, turns, pieces, values, splits, transpose, name, vmem=40 << 20):
    _, block, _ = values.shape
    width = pieces[0].shape[-1]
    pieces = [piece.reshape(-1, block, width) for piece in pieces]
    n_src = sum(piece.shape[0] for piece in pieces)
    n_dst = sum(count for count, _ in splits)
    n_rounded = sum(count for count, kind in splits if kind != F32)
    anywhere = pl.BlockSpec(memory_space=pl.ANY)
    return pl.pallas_call(
        functools.partial(tile_kernel, transpose, len(pieces), splits),
        grid_spec=pltpu.PrefetchScalarGridSpec(
            num_scalar_prefetch=3,
            grid=(1,),
            in_specs=[anywhere] * (len(pieces) + 1),
            out_specs=[anywhere] * len(splits),
            scratch_shapes=[
                pltpu.VMEM((n_src, block, width), BF),
                pltpu.VMEM((DEPTH * UNROLL, block, block), BF),
                pltpu.VMEM((n_dst + 1, block, width), F32),
                pltpu.VMEM((n_rounded, block, width), BF),
                pltpu.SemaphoreType.DMA((len(pieces),)),
                pltpu.SemaphoreType.DMA((DEPTH,)),
                pltpu.SemaphoreType.DMA((len(splits),)),
            ],
        ),
        out_shape=[jax.ShapeDtypeStruct((count, block, width), kind) for count, kind in splits],
        compiler_params=pltpu.CompilerParams(vmem_limit_bytes=vmem),
        cost_estimate=pl.CostEstimate(flops=18_000_000_000, bytes_accessed=20 << 20, transcendentals=0),
        name=name,
    )(src, dst, turns, *pieces, values)


def add_cores(own, other):
    width = own.shape[-1]

    def part(d):
        return (own[8 * d : 8 * d + 8] + other[8 * d : 8 * d + 8].astype(F32)).reshape(-1, width)

    return part(0), [part(d).astype(BF) for d in (1, 3, 2)]


def send_x(parts):
    return [send_col(part, d, 0) for part, d in zip(parts, (1, 3, 2))]


def add_x(own, sent):
    total = own + sent[0].astype(F32) + sent[1].astype(F32) + sent[2].astype(F32)
    return total.reshape(2, -1, total.shape[-1])


def add_z(halves):
    return halves[0] + send_col(halves[1].astype(BF), 0, 1).astype(F32)


def add_z_hi(own, sent):
    other = jnp.concatenate(sent).astype(F32)
    return (own + other).reshape(4, -1, own.shape[-1])


def sum_y(parts):
    sent = [send_row(parts[d].astype(BF), d, 0) for d in (1, 3, 2)]
    return parts[0] + sent[0].astype(F32) + sent[1].astype(F32) + sent[2].astype(F32)


def pick(parts, i):
    return lax.dynamic_index_in_dim(parts, i, 0, False)


def sum_cores(value, core):
    halves = value.reshape(2, -1, value.shape[-1])
    return pick(halves, core) + send_col(pick(halves, 1 - core), 0, 0, 1)


def scatter_x(part, x):
    parts = part.reshape(4, -1, part.shape[-1])
    sent = [send_col(pick(parts, (x + d) % 4), d, 0) for d in (2, 1, 3)]
    return pick(parts, x) + sent[0] + sent[1] + sent[2]


def exchange_y(part):
    far, above, below = [send_row(part, d, 0) for d in (2, 1, 3)]
    return (part + far) + (above + below)


def exchange_z(part):
    high, low, both = send_row(part, 0, 1), send_col(part, 0, 1), send_both_z(part)
    return (part + high) + (low + both)


def gather_x(part, x):
    far, above, below = [send_col(part, d, 0) for d in (2, 1, 3)]
    parts = jnp.stack([part, above, far, below])
    return jnp.concatenate([pick(parts, (x - j) % 4) for j in range(4)])


def fdot(left, right):
    return jnp.dot(left, right.astype(F32), precision=lax.Precision.HIGHEST, preferred_element_type=F32)


def local(
    features,
    cotangent,
    w_self1,
    w_neigh1,
    w_self2,
    w_neigh2,
    tile_rows,
    tile_cols,
    tile_values,
    tile_live,
):
    values = tile_values[0, 0]
    slots = values.shape[0]
    live = tile_live[0, 0]
    rows_here = tile_rows[0, 0]
    cols_here = tile_cols[0, 0]
    row_at = lax.axis_index("row")
    col_at = lax.axis_index("col")
    y, z_hi = row_at // 2, row_at % 2
    z_lo, x, core = col_at // 8, (col_at // 2) % 4, col_at % 2

    owner = cols_here // 4
    dy = (owner // 2 - y) % 4
    dz = (owner % 2) ^ z_hi
    place = jnp.where(dy == 0, 0, jnp.where(dy == 3, 2, jnp.where(dy == 1, 4, 6))) + dz
    col_place = place * 4 + cols_here % 4
    col_sum_place = dz * 16 + dy * 4 + cols_here % 4
    owner = rows_here // 4
    dx = ((owner // 2) % 4 - x) % 4
    dz = (owner // 8) ^ z_lo
    row_place = ((owner % 2) ^ core) * 32 + (dx * 2 + dz) * 4 + rows_here % 4
    alive = jnp.arange(slots, dtype=jnp.int32) < live
    row_target = jnp.where(alive, row_place, 64)
    col_target = jnp.where(alive, col_sum_place, 32)
    turns = ((live + UNROLL - 1) // UNROLL).reshape(1)

    forward_splits = ((32, F32), (32, BF))
    back_splits = ((16, F32), (8, BF), (8, BF))

    gathered_c = lax.all_gather(cotangent, "col", axis=0, tiled=True)
    gathered_x = gather_row(features)
    own, other = tile_product(
        col_place, row_target, turns, gathered_x, values, forward_splits, False, "neighbour_sum_one"
    )
    mine, parts = add_cores(own, send_col(other, 0, 0, 1))
    last, gathered_c = lax.optimization_barrier((parts[2], gathered_c))
    sent = send_x([parts[0], parts[1], last])
    back_own, *back_parts = tile_product(
        rows_here, col_target, turns, [gathered_c], values, back_splits, True, "neighbour_sum_back"
    )
    sent, back_parts = lax.optimization_barrier((sent, back_parts))
    back_parts = [send_row(part, 0, 1) for part in back_parts]
    agg1 = add_z(add_x(mine, sent))
    z1 = jnp.dot(features, w_self1, preferred_element_type=F32) + fdot(agg1, w_neigh1)
    h1 = jax.nn.silu(z1).astype(BF)
    gathered_h = gather_row(h1)
    gathered_h, back_parts = lax.optimization_barrier((gathered_h, back_parts))
    back_parts = add_z_hi(back_own, back_parts)
    gathered_h, back_parts = lax.optimization_barrier((gathered_h, back_parts))
    back = sum_y(back_parts)
    own, other = tile_product(
        col_place, row_target, turns, gathered_h, values, forward_splits, False, "neighbour_sum_two"
    )
    own, other, back = lax.optimization_barrier((own, other, back))
    other = send_col(other, 0, 0, 1)
    dh1 = jnp.dot(cotangent, w_self2.T, preferred_element_type=F32) + fdot(back, w_neigh2.T)
    sigma = jax.nn.sigmoid(z1)
    dz1 = (dh1 * (sigma + z1 * sigma * (1.0 - sigma))).astype(BF)
    local_self2 = jnp.dot(h1.T, cotangent, preferred_element_type=F32)
    local_neigh2 = jnp.dot(
        h1.T.astype(F32), back, precision=lax.Precision.HIGHEST, preferred_element_type=F32
    )
    local_self1 = jnp.dot(features.T, dz1, preferred_element_type=F32)
    local_neigh1 = fdot(agg1.T, dz1)
    grads = jnp.concatenate([local_self1, local_neigh1, local_self2, local_neigh2])
    mine, parts = add_cores(own, other)
    sent = send_x(parts)
    grads = exchange_y(scatter_x(sum_cores(grads, core), x))
    sent, grads = lax.optimization_barrier((sent, grads))
    grads = exchange_z(grads)
    agg2 = add_z(add_x(mine, sent))
    output = (jnp.dot(h1, w_self2, preferred_element_type=F32) + fdot(agg2, w_neigh2)).astype(BF)
    grads = gather_x(grads, x)
    other = send_col(grads, 0, 0, 1)
    grads = jnp.where(core == 0, jnp.concatenate([grads, other]), jnp.concatenate([other, grads]))
    return (output, grads[:128], grads[128:256], grads[256:512], grads[512:])


def solution(mesh):
    return jax.shard_map(
        local,
        mesh=mesh,
        in_specs=(
            P(("row", "col"), None),
            P(("row", "col"), None),
            P(),
            P(),
            P(),
            P(),
            P("row", "col", None),
            P("row", "col", None),
            P("row", "col", None, None, None),
            P("row", "col"),
        ),
        out_specs=(P(("row", "col"), None), P(), P(), P(), P()),
        check_vma=False,
    )
```

```python
import functools

import jax
import jax.numpy as jnp
from jax import lax
from jax.experimental import pallas as pl
from jax.experimental.pallas import tpu as pltpu
from jax.sharding import PartitionSpec as P

BF = jnp.bfloat16
F32 = jnp.float32
UNROLL = 56
DEPTH = 3


def row_perm(dy, dz):
    return [(y * 2 + h, ((y + dy) % 4) * 2 + (h ^ dz)) for y in range(4) for h in range(2)]


def col_perm(dx, dz, dc):
    return [
        ((z * 4 + x) * 2 + c, ((z ^ dz) * 4 + (x + dx) % 4) * 2 + (c ^ dc))
        for z in range(2)
        for x in range(4)
        for c in range(2)
    ]


def send_both_z(value):
    pairs = [(r * 16 + c, (r ^ 1) * 16 + (c ^ 8)) for r in range(8) for c in range(16)]
    return lax.ppermute(value, ("row", "col"), pairs)


def send_row(value, dy, dz):
    return lax.ppermute(value, "row", row_perm(dy, dz))


def send_col(value, dx, dz, dc=0):
    return lax.ppermute(value, "col", col_perm(dx, dz, dc))


def gather_row(value):
    pair = jnp.concatenate([value, send_row(value, 0, 1)])
    below, above, far = [send_row(pair, dy, 0) for dy in (1, 3, 2)]
    return [pair, below, above, far]


def tile_kernel(transpose, n_pieces, splits, *refs):
    src, dst, turns = refs[:3]
    pieces = refs[3 : 3 + n_pieces]
    values = refs[3 + n_pieces]
    outs = refs[4 + n_pieces : 4 + n_pieces + len(splits)]
    held, ring, total, rounded, piece_sems, ring_sems, out_sems = refs[4 + n_pieces + len(splits) :]
    count = turns[0]

    def fetch(turn, slot):
        return pltpu.make_async_copy(
            values.at[pl.ds(turn * UNROLL, UNROLL)], ring.at[pl.ds(slot * UNROLL, UNROLL)], ring_sems.at[slot]
        )

    copies = []
    at = 0
    for k, piece in enumerate(pieces):
        copy = pltpu.make_async_copy(piece, held.at[pl.ds(at, piece.shape[0])], piece_sems.at[k])
        copy.start()
        copies.append(copy)
        at += piece.shape[0]
    for slot in range(DEPTH):

        @pl.when(slot < count)
        def _():
            fetch(slot, slot).start()

    def clear(i, carry):
        total[i] = jnp.zeros(total.shape[1:], F32)
        return carry

    lax.fori_loop(0, total.shape[0], clear, 0)
    for copy in copies:
        copy.wait()

    def body(turn, carry):
        slot = lax.rem(turn, DEPTH)
        fetch(turn, slot).wait()
        for u in range(UNROLL):
            s = src[turn * UNROLL + u]
            d = dst[turn * UNROLL + u]
            dims = (((0,), (0,)), ((), ())) if transpose else (((1,), (0,)), ((), ()))
            total[d] += lax.dot_general(ring[slot * UNROLL + u], held[s], dims, preferred_element_type=F32)

        @pl.when(turn + DEPTH < count)
        def _():
            fetch(turn + DEPTH, slot).start()

        return carry

    lax.fori_loop(0, count, body, 0)

    copies = []
    at = 0
    for k, (out, (blocks, kind)) in enumerate(zip(outs, splits)):
        if kind == F32:
            copies.append(pltpu.make_async_copy(total.at[pl.ds(at, blocks)], out, out_sems.at[k]))
            copies[-1].start()
        at += blocks
    at = 0
    to = 0
    for k, (out, (blocks, kind)) in enumerate(zip(outs, splits)):
        if kind != F32:

            def cast(i, carry, at=at, to=to):
                rounded[to + i] = total[at + i].astype(BF)
                return carry

            lax.fori_loop(0, blocks, cast, 0)
            copies.append(pltpu.make_async_copy(rounded.at[pl.ds(to, blocks)], out, out_sems.at[k]))
            copies[-1].start()
            to += blocks
        at += blocks
    for copy in copies:
        copy.wait()


def tile_product(src, dst, turns, pieces, values, splits, transpose, name, vmem=40 << 20):
    _, block, _ = values.shape
    width = pieces[0].shape[-1]
    pieces = [piece.reshape(-1, block, width) for piece in pieces]
    n_src = sum(piece.shape[0] for piece in pieces)
    n_dst = sum(count for count, _ in splits)
    n_rounded = sum(count for count, kind in splits if kind != F32)
    anywhere = pl.BlockSpec(memory_space=pl.ANY)
    return pl.pallas_call(
        functools.partial(tile_kernel, transpose, len(pieces), splits),
        grid_spec=pltpu.PrefetchScalarGridSpec(
            num_scalar_prefetch=3,
            grid=(1,),
            in_specs=[anywhere] * (len(pieces) + 1),
            out_specs=[anywhere] * len(splits),
            scratch_shapes=[
                pltpu.VMEM((n_src, block, width), BF),
                pltpu.VMEM((DEPTH * UNROLL, block, block), BF),
                pltpu.VMEM((n_dst + 1, block, width), F32),
                pltpu.VMEM((n_rounded, block, width), BF),
                pltpu.SemaphoreType.DMA((len(pieces),)),
                pltpu.SemaphoreType.DMA((DEPTH,)),
                pltpu.SemaphoreType.DMA((len(splits),)),
            ],
        ),
        out_shape=[jax.ShapeDtypeStruct((count, block, width), kind) for count, kind in splits],
        compiler_params=pltpu.CompilerParams(vmem_limit_bytes=vmem),
        cost_estimate=pl.CostEstimate(flops=18_000_000_000, bytes_accessed=20 << 20, transcendentals=0),
        name=name,
    )(src, dst, turns, *pieces, values)


def add_cores(own, other):
    width = own.shape[-1]

    def part(d):
        return (own[8 * d : 8 * d + 8] + other[8 * d : 8 * d + 8].astype(F32)).reshape(-1, width)

    return part(0), [part(d).astype(BF) for d in (1, 3, 2)]


def send_x(parts):
    return [send_col(part, d, 0) for part, d in zip(parts, (1, 3, 2))]


def add_x(own, sent):
    total = own + sent[0].astype(F32) + sent[1].astype(F32) + sent[2].astype(F32)
    return total.reshape(2, -1, total.shape[-1])


def add_z(halves):
    return halves[0] + send_col(halves[1].astype(BF), 0, 1).astype(F32)


def add_z_hi(own, sent):
    other = jnp.concatenate(sent).astype(F32)
    return (own + other).reshape(4, -1, own.shape[-1])


def sum_y(parts):
    sent = [send_row(parts[d].astype(BF), d, 0) for d in (1, 3, 2)]
    return parts[0] + sent[0].astype(F32) + sent[1].astype(F32) + sent[2].astype(F32)


def pick(parts, i):
    return lax.dynamic_index_in_dim(parts, i, 0, False)


def sum_cores(value, core):
    halves = value.reshape(2, -1, value.shape[-1])
    return pick(halves, core) + send_col(pick(halves, 1 - core), 0, 0, 1)


def scatter_x(part, x):
    parts = part.reshape(4, -1, part.shape[-1])
    sent = [send_col(pick(parts, (x + d) % 4), d, 0) for d in (1, 3, 2)]
    return pick(parts, x) + sent[0] + sent[1] + sent[2]


def exchange_y(part):
    above, below, far = [send_row(part, d, 0) for d in (1, 3, 2)]
    return (part + far) + (above + below)


def exchange_z(part):
    high, low, both = send_row(part, 0, 1), send_col(part, 0, 1), send_both_z(part)
    return (part + high) + (low + both)


def gather_x(part, x):
    above, below, far = [send_col(part, d, 0) for d in (1, 3, 2)]
    parts = jnp.stack([part, above, far, below])
    return jnp.concatenate([pick(parts, (x - j) % 4) for j in range(4)])


def fdot(left, right):
    return jnp.dot(left, right.astype(F32), precision=lax.Precision.HIGHEST, preferred_element_type=F32)


def local(
    features,
    cotangent,
    w_self1,
    w_neigh1,
    w_self2,
    w_neigh2,
    tile_rows,
    tile_cols,
    tile_values,
    tile_live,
):
    values = tile_values[0, 0]
    slots = values.shape[0]
    live = tile_live[0, 0]
    rows_here = tile_rows[0, 0]
    cols_here = tile_cols[0, 0]
    row_at = lax.axis_index("row")
    col_at = lax.axis_index("col")
    y, z_hi = row_at // 2, row_at % 2
    z_lo, x, core = col_at // 8, (col_at // 2) % 4, col_at % 2

    owner = cols_here // 4
    dy = (owner // 2 - y) % 4
    dz = (owner % 2) ^ z_hi
    place = jnp.where(dy == 0, 0, jnp.where(dy == 3, 2, jnp.where(dy == 1, 4, 6))) + dz
    col_place = place * 4 + cols_here % 4
    col_sum_place = dz * 16 + dy * 4 + cols_here % 4
    owner = rows_here // 4
    dx = ((owner // 2) % 4 - x) % 4
    dz = (owner // 8) ^ z_lo
    row_place = ((owner % 2) ^ core) * 32 + (dx * 2 + dz) * 4 + rows_here % 4
    alive = jnp.arange(slots, dtype=jnp.int32) < live
    row_target = jnp.where(alive, row_place, 64)
    col_target = jnp.where(alive, col_sum_place, 32)
    turns = ((live + UNROLL - 1) // UNROLL).reshape(1)

    forward_splits = ((32, F32), (32, BF))
    back_splits = ((16, F32), (8, BF), (8, BF))

    gathered_c = lax.all_gather(cotangent, "col", axis=0, tiled=True)
    gathered_x = gather_row(features)
    own, other = tile_product(
        col_place, row_target, turns, gathered_x, values, forward_splits, False, "neighbour_sum_one"
    )
    mine, parts = add_cores(own, send_col(other, 0, 0, 1))
    last, gathered_c = lax.optimization_barrier((parts[2], gathered_c))
    sent = send_x([parts[0], parts[1], last])
    back_own, *back_parts = tile_product(
        rows_here, col_target, turns, [gathered_c], values, back_splits, True, "neighbour_sum_back"
    )
    sent, back_parts = lax.optimization_barrier((sent, back_parts))
    back_parts = [send_row(part, 0, 1) for part in back_parts]
    agg1 = add_z(add_x(mine, sent))
    z1 = jnp.dot(features, w_self1, preferred_element_type=F32) + fdot(agg1, w_neigh1)
    h1 = jax.nn.silu(z1).astype(BF)
    gathered_h = gather_row(h1)
    gathered_h, back_parts = lax.optimization_barrier((gathered_h, back_parts))
    back_parts = add_z_hi(back_own, back_parts)
    gathered_h, back_parts = lax.optimization_barrier((gathered_h, back_parts))
    back = sum_y(back_parts)
    own, other = tile_product(
        col_place, row_target, turns, gathered_h, values, forward_splits, False, "neighbour_sum_two"
    )
    own, other, back = lax.optimization_barrier((own, other, back))
    other = send_col(other, 0, 0, 1)
    dh1 = jnp.dot(cotangent, w_self2.T, preferred_element_type=F32) + fdot(back, w_neigh2.T)
    sigma = jax.nn.sigmoid(z1)
    dz1 = (dh1 * (sigma + z1 * sigma * (1.0 - sigma))).astype(BF)
    local_self2 = jnp.dot(h1.T, cotangent, preferred_element_type=F32)
    local_neigh2 = jnp.dot(
        h1.T.astype(F32), back, precision=lax.Precision.HIGHEST, preferred_element_type=F32
    )
    local_self1 = jnp.dot(features.T, dz1, preferred_element_type=F32)
    local_neigh1 = fdot(agg1.T, dz1)
    grads = jnp.concatenate([local_self1, local_self2, local_neigh1, local_neigh2])
    mine, parts = add_cores(own, other)
    sent = send_x(parts)
    grads = exchange_y(scatter_x(sum_cores(grads, core), x))
    sent, grads = lax.optimization_barrier((sent, grads))
    grads = exchange_z(grads)
    agg2 = add_z(add_x(mine, sent))
    output = (jnp.dot(h1, w_self2, preferred_element_type=F32) + fdot(agg2, w_neigh2)).astype(BF)
    grads = gather_x(grads, x)
    other = send_col(grads, 0, 0, 1)
    own_first = core == 0
    grads_self = jnp.where(own_first, grads, other)
    grads_neigh = jnp.where(own_first, other, grads)
    return (output, grads_self[:128], grads_neigh[:128], grads_self[128:], grads_neigh[128:])


def solution(mesh):
    return jax.shard_map(
        local,
        mesh=mesh,
        in_specs=(
            P(("row", "col"), None),
            P(("row", "col"), None),
            P(),
            P(),
            P(),
            P(),
            P("row", "col", None),
            P("row", "col", None),
            P("row", "col", None, None, None),
            P("row", "col"),
        ),
        out_specs=(P(("row", "col"), None), P(), P(), P(), P()),
        check_vma=False,
    )
```
